512 devices in a mesh: seq: 64 (over z, x_hi, core), mp: 8 (over y, x_lo).
Axes of the slice: x: 4 (x_hi: 2, x_lo: 2; x = x_hi * 2 + x_lo), y: 4, z: 16, core: 2. Of those that a mesh axis runs over, the one named last changes fastest.
Arguments:
- query_branch: bfloat16 [16384, 4096], P('seq', 'mp'), may hold values from -6 to 6
- key_branch: bfloat16 [16384, 4096], P('seq', 'mp'), may hold values from -6 to 6
- value_branch: bfloat16 [16384, 4096], P('seq', 'mp'), may hold values from -6 to 6
- long_filter: bfloat16 [16384, 4096], P('seq', 'mp'), may hold values from -0.046875 to 0.046875
- cotangent: bfloat16 [16384, 2048], P('seq', 'mp'), may hold values from -16 to 16
- out_weight: bfloat16 [2048, 4096], P('seq', 'mp'), may hold values from -0.125 to 0.125
Outputs:
- grad_query: bfloat16 [16384, 4096], P('seq', 'mp')
- grad_key: bfloat16 [16384, 4096], P('seq', 'mp')
- grad_value: bfloat16 [16384, 4096], P('seq', 'mp')
- grad_filter: bfloat16 [16384, 4096], P('seq', 'mp')
- grad_out_weight: float32 [2048, 4096], P('seq', 'mp')
The draws below stay inside these ranges and needn't reach their ends.
All inputs are finite; a program needn't handle non-finite values.
Results may differ from the reference program's by a relative error of at most 0.015.
Values may be sent and summed in bfloat16 or wider, within the bound.
A program may use at most 128 MiB of HBM per device.

```python
import math
import jax
import jax.numpy as jnp
from jax import lax

D = 4096
DOUT = 2048
SEQLEN = 16384


def strengthened(array, key, source, target, shards_of, factor):
    owner, partner = [(jnp.arange(array.shape[position]) // (array.shape[position] // shards_of)).reshape([-1 if axis == position else 1 for axis in range(array.ndim)]) for position in (source, target)]
    chosen = jax.random.permutation(key, shards_of)[partner]
    strong = (owner == chosen) | (owner == (partner + shards_of // 2) % shards_of)
    return jnp.where(strong, factor * array, array)


def block_levels(rng, shape, pieces, smallest, top_value):
    def one(position, blocks):
        heights = jax.random.uniform(jax.random.fold_in(jax.random.fold_in(rng, 6), position), (blocks,), jnp.float32, smallest / len(pieces), top_value / len(pieces))
        return jnp.repeat(jnp.exp(heights), shape[position] // blocks).reshape((-1,) + (1,) * (len(shape) - position - 1))

    gain = one(*pieces[0])
    for cut in pieces[1:]:
        gain = gain * one(*cut)
    return gain


def scatter_about(key, extent, spread, reach, pieces=(), held_as=jnp.bfloat16):
    loudness = block_levels(key, extent, pieces, -0.22, 0.18) if pieces else 1.0
    result = jax.random.normal(key, extent, jnp.float32) * spread * loudness
    return jnp.minimum(jnp.maximum(result, -reach), reach).astype(held_as)


def bell_draw_with(key, extent, width, reach, shards, heavy, kind=jnp.bfloat16):
    drawn = width * jax.random.normal(key, extent, jnp.float32)
    if shards:
        drawn = drawn * block_levels(key, extent, shards, -0.22, 0.18)
    return jnp.clip(strengthened(drawn, jax.random.fold_in(key, 3), *heavy), -reach, reach).astype(kind)


def setup_inputs(seed: int = 0) -> dict:
    splits = jax.random.split(jax.random.key(seed), 7)
    return {
        "query_branch": scatter_about(splits[0], (SEQLEN, D), 1.0, 6.0, ((0, 64), (1, 8))),
        "key_branch": scatter_about(splits[1], (SEQLEN, D), 1.0, 6.0, ((0, 64), (1, 8))),
        "value_branch": scatter_about(splits[2], (SEQLEN, D), 1.0, 6.0, ((0, 64), (1, 8))),
        "long_filter": scatter_about(splits[3], (SEQLEN, D), SEQLEN ** -0.5, 0.046875, ((0, 64), (1, 8))),
        "cotangent": bell_draw_with(splits[4], (SEQLEN, DOUT), 1.0, 16.0, ((0, 64), (1, 8)), (0, 1, 64, 4.0)),
        "out_weight": scatter_about(splits[5], (DOUT, D), DOUT ** -0.5, 0.125, ((0, 64), (1, 8))),
    }


def block_forward(pair):
    filt_block, input_block = pair
    total = 2 * SEQLEN
    spec_filter = jnp.fft.fft(filt_block, n=total, axis=-1)
    spec_input = jnp.fft.fft(input_block, n=total, axis=-1)
    return jnp.real(jnp.fft.ifft(spec_filter * spec_input, axis=-1))[:, :SEQLEN]

def block_backward(triple):
    filt_block, input_block, grad_block = triple
    total = 2 * SEQLEN
    spec_filter = jnp.fft.fft(filt_block, n=total, axis=-1)
    spec_input = jnp.fft.fft(input_block, n=total, axis=-1)
    spec_grad = jnp.fft.fft(grad_block, n=total, axis=-1)
    grad_in = jnp.real(jnp.fft.ifft(jnp.conj(spec_filter) * spec_grad, axis=-1))[:, :SEQLEN]
    grad_taps = jnp.real(jnp.fft.ifft(jnp.conj(spec_input) * spec_grad, axis=-1))[:, :SEQLEN]
    return (grad_in, grad_taps)

def reference(query_branch, key_branch, value_branch, long_filter, cotangent, out_weight):
    block = math.gcd(D, 512)
    count = D // block

    def to_blocks(field):
        return field.astype(jnp.float32).T.reshape(count, block, SEQLEN)

    def from_blocks(field):
        return field.reshape(D, SEQLEN).T
    grad_scale = 1.0 / math.sqrt(SEQLEN)
    query = query_branch.astype(jnp.float32)
    keys = key_branch.astype(jnp.float32)
    values = value_branch.astype(jnp.float32)
    gated_input = (keys * values).astype(jnp.bfloat16)
    filt_blocks = to_blocks(long_filter)
    input_blocks = to_blocks(gated_input)
    conv_out = from_blocks(lax.map(block_forward, (filt_blocks, input_blocks))).astype(jnp.bfloat16)
    grad_gated = jnp.dot(cotangent, out_weight, preferred_element_type=jnp.float32).astype(jnp.bfloat16)
    conv_wide = conv_out.astype(jnp.float32)
    gated_out = (query * conv_wide).astype(jnp.bfloat16)
    grad_out_weight = jnp.dot(cotangent.T, gated_out, preferred_element_type=jnp.float32) * grad_scale
    grad_wide = grad_gated.astype(jnp.float32)
    grad_query = (grad_wide * conv_wide).astype(jnp.bfloat16)
    grad_conv = (grad_wide * query).astype(jnp.bfloat16)
    grad_in, grad_taps = lax.map(block_backward, (filt_blocks, input_blocks, to_blocks(grad_conv)))
    grad_input = from_blocks(grad_in).astype(jnp.bfloat16).astype(jnp.float32)
    grad_filter = (from_blocks(grad_taps) * grad_scale).astype(jnp.bfloat16)
    grad_key = (grad_input * values).astype(jnp.bfloat16)
    grad_value = (grad_input * keys).astype(jnp.bfloat16)
    return (grad_query, grad_key, grad_value, grad_filter, grad_out_weight)
```

```python
import functools
import math

import jax
import jax.numpy as jnp
import numpy as np
from jax import lax
from jax.experimental import pallas as pl
from jax.experimental.pallas import tpu as pltpu
from jax.sharding import PartitionSpec as P

MESH = pl.DeviceIdType.MESH
BF16 = jnp.bfloat16
F32 = jnp.float32
QUAD = 4


def tables(blocks, width, group):
    points = blocks * width
    block = np.arange(blocks)
    lane = np.arange(width)
    turn_block = 2.0 * np.pi * (np.outer(block, 4 * block + 1) % (4 * blocks)) / (4 * blocks)
    turn_mix = 2.0 * np.pi * np.outer(4 * block + 1, lane) / (4 * points)
    turn_lane = 2.0 * np.pi * (np.outer(lane, lane) % width) / width
    cos_l, sin_l = np.cos(turn_lane), np.sin(turn_lane)
    first = np.concatenate([np.cos(turn_block.T), -np.sin(turn_block.T)], axis=0)
    last = np.concatenate([np.cos(turn_block), -np.sin(turn_block)], axis=1) / points
    return (
        jnp.asarray(np.repeat(first, group, axis=1), F32),
        jnp.asarray(np.repeat(last, group, axis=0), F32),
        jnp.asarray(np.cos(turn_mix), F32),
        jnp.asarray(-np.sin(turn_mix), F32),
        jnp.asarray(np.block([[cos_l, -sin_l], [sin_l, cos_l]]), BF16),
        jnp.asarray(np.block([[cos_l, sin_l], [-sin_l, cos_l]]), BF16),
    )


def dot(left, right):
    return jnp.dot(left, right, preferred_element_type=F32)


def pack(field, blocks, group):
    half = field.shape[1] // 2
    shaped = field.reshape(blocks, group, 2 * half)
    return jnp.concatenate([shaped[:, :, :half], shaped[:, :, half:]], axis=1)


def unpack(packed, blocks, group):
    wide = packed.astype(F32)
    joined = jnp.concatenate([wide[:, :group], wide[:, group:]], axis=2)
    return joined.reshape(blocks * group, joined.shape[2])


def product(left, right, conjugate):
    width = left.shape[1] // 2
    left_re, left_im = left[:, :width], left[:, width:]
    right_re, right_im = right[:, :width], right[:, width:]
    if conjugate:
        return jnp.concatenate(
            [left_re * right_re + left_im * right_im, left_re * right_im - left_im * right_re], axis=1
        )
    return jnp.concatenate(
        [left_re * right_re - left_im * right_im, left_re * right_im + left_im * right_re], axis=1
    )


def body(
    sizes,
    query_ref, key_ref, value_ref, filter_ref, cot_ref, weight_ref,
    first_ref, last_ref, mix_re_ref, mix_im_ref, lane_ref, lane_back_ref,
    grad_query_ref, grad_key_ref, grad_value_ref, grad_filter_ref, grad_weight_ref,
    out_a, in_a, out_g, in_g, out_c, in_c, out_d, in_d,
    first_wide, last_wide, spec_f, spec_x,
    weights, cots, cots_t, part, core_in, pair_out, pair_in, mine, down_out, down_in, up_out, up_in,
    a2a_sems, w_send, w_down, w_up, w_pair, w_core, cot_send, cot_pair, cot_near, cot_far,
    r_send, r_core, r_pair, r_down, r_up,
):
    seq, mps, blocks, width, group = sizes
    depth = seq // QUAD
    half = depth // 2
    columns = mps // 2
    scale = 1.0 / math.sqrt(blocks * width)
    me, mp = lax.axis_index("seq"), lax.axis_index("mp")
    z, quad = me // QUAD, lax.rem(me, QUAD)
    core_peer = me + 1 - 2 * lax.rem(quad, 2)
    pair_quad = lax.rem(quad + 2, QUAD)
    pair_peer = z * QUAD + pair_quad
    up = lax.rem(z + 1, depth) * QUAD + quad
    down = lax.rem(z + depth - 1, depth) * QUAD + quad

    def on_seq(peer):
        return (peer, mp)

    def on_mp(peer):
        return (me, peer)

    def peer_of(step):
        return lax.rem(me + step + 1, seq)

    def remote(source, target, send, receive, device):
        return pltpu.make_async_remote_copy(
            src_ref=source, dst_ref=target, send_sem=send, recv_sem=receive,
            device_id=device, device_id_type=MESH,
        )

    def whole_wait(ref, sem):
        pltpu.make_async_copy(ref, ref, sem).wait()

    barrier = pltpu.get_barrier_semaphore()

    @pl.loop(0, seq - 1)
    def _(step):
        pl.semaphore_signal(barrier, inc=1, device_id=on_seq(peer_of(step)), device_id_type=MESH)

    @pl.loop(0, mps - 1)
    def _(step):
        pl.semaphore_signal(barrier, inc=1, device_id=on_mp(lax.rem(mp + step + 1, mps)), device_id_type=MESH)

    def a2a_start(source, target, index):
        pltpu.make_async_copy(source.at[me], target.at[me], a2a_sems.at[index, 2]).start()

        @pl.loop(0, seq - 1)
        def _(step):
            back = seq - 2 - step
            away = back // 2 + 1
            offset = jnp.where(lax.rem(back, 2) == 0, away, seq - away)
            peer = lax.rem(me + offset, seq)
            remote(
                source.at[peer], target.at[me], a2a_sems.at[index, 0], a2a_sems.at[index, 1], on_seq(peer)
            ).start()

    def a2a_wait(source, target, index):
        pltpu.make_async_copy(source.at[me], target.at[me], a2a_sems.at[index, 2]).wait()
        rest = pl.ds(0, seq - 1)
        pltpu.make_async_copy(target.at[rest], target.at[rest], a2a_sems.at[index, 1]).wait()

    def a2a_sent(source, index):
        rest = pl.ds(0, seq - 1)
        pltpu.make_async_copy(source.at[rest], source.at[rest], a2a_sems.at[index, 0]).wait()

    gated = (key_ref[...].astype(F32) * value_ref[...].astype(F32)).astype(BF16).astype(F32)
    taps = filter_ref[...].astype(F32)
    out_a[...] = jnp.concatenate(
        [pack(gated.T, seq, group), pack(taps.T, seq, group)], axis=1
    ).astype(BF16)

    rows = 2 * blocks
    lane_group = lax.rem(lax.broadcasted_iota(jnp.int32, (rows, blocks * group), 1), group)
    row_group = lax.rem(lax.broadcasted_iota(jnp.int32, (blocks * group, rows), 0), group)
    for channel in range(group):
        first_wide[pl.ds(channel * rows, rows), :] = jnp.where(
            lane_group == channel, first_ref[...], 0.0
        ).astype(BF16)
        last_wide[:, pl.ds(channel * rows, rows)] = jnp.where(
            row_group == channel, last_ref[...], 0.0
        ).astype(BF16)

    pl.semaphore_wait(barrier, seq - 1 + mps - 1)

    weights[z, quad] = weight_ref[...]
    cots[mp] = cot_ref[...]

    def ring_up(step):
        at = weights.at[lax.rem(z + depth - step, depth), quad]
        return remote(at, at, w_send.at[0], w_up.at[step], on_seq(up))

    def ring_down(step):
        at = weights.at[lax.rem(z + step, depth), quad]
        return remote(at, at, w_send.at[1], w_down.at[step], on_seq(down))

    def cot_copy(block, peer, send, receive):
        return remote(cots.at[block], cots.at[block], send, receive, on_mp(peer))

    mp_pair = mp + 1 - 2 * lax.rem(mp, 2)

    def along(step, block):
        return lax.rem(mp + 2 * (step + 1), mps), lax.rem(block + mps, mps)

    ring_up(0).start()
    ring_down(0).start()
    cot_copy(mp, mp_pair, cot_send.at[0], cot_pair.at[0]).start()
    for step in range(columns - 1):
        peer = lax.rem(mp + 2 * (step + 1), mps)
        cot_copy(mp, peer, cot_send.at[1 + step], cot_near.at[step]).start()
    a2a_start(out_a, in_a, 0)

    def pair_copy(origin):
        at = weights.at[origin, quad]
        return remote(at, at, w_send.at[2], w_pair.at[0], on_seq(pair_peer))

    pair_copy(z).start()
    for step in range(half):
        from_below = lax.rem(z + depth - step - 1, depth)
        from_above = lax.rem(z + step + 1, depth)
        ring_up(step).wait_recv()
        if step + 1 < half:
            ring_up(step + 1).start()
        pair_copy(from_below).start()
        if step < half - 1:
            ring_down(step).wait_recv()
            if step + 1 < half - 1:
                ring_down(step + 1).start()
            pair_copy(from_above).start()
        if step == 0:
            cot_copy(mp, mp_pair, cot_send.at[0], cot_pair.at[0]).wait_recv()
            for hop in range(columns - 1):
                peer = lax.rem(mp + 2 * (hop + 1), mps)
                cot_copy(mp_pair, peer, cot_send.at[columns + hop], cot_far.at[hop]).start()

    def core_copy(which, slot):
        at = weights.at[:, which]
        return remote(at, at, w_send.at[3 + slot], w_core.at[slot], on_seq(core_peer))

    core_copy(quad, 0).start()
    whole_wait(weights.at[:, pair_quad], w_pair.at[0])
    core_copy(pair_quad, 1).start()
    for hop in range(columns - 1):
        cot_copy(mp, mp, cot_send.at[1 + hop], cot_near.at[hop]).wait_recv()
        cot_copy(mp, mp, cot_send.at[columns + hop], cot_far.at[hop]).wait_recv()
    for block in range(mps):
        cots_t[block] = cots[block].astype(F32).T.astype(BF16)
    core_copy(quad, 0).wait_recv()
    core_copy(pair_quad, 1).wait_recv()

    features = cots.shape[2]
    quad_rows = weights.shape[2]
    per_block = features // (QUAD * quad_rows)
    total = jnp.zeros(query_ref.shape, F32)
    for block in range(mps):
        piece = weights[pl.ds(block * per_block, per_block)].reshape(features, query_ref.shape[1])
        total = total + dot(cots[block], piece)
    grad_gated = total.astype(BF16).astype(F32)
    grad_query_ref[...] = grad_gated.astype(BF16)
    query = query_ref[...].astype(F32)
    grad_conv = (grad_gated * query).astype(BF16).astype(F32)
    out_g[...] = pack(grad_conv.T, seq, group).astype(BF16)
    a2a_start(out_g, in_g, 1)

    mix_re, mix_im = mix_re_ref[...], mix_im_ref[...]

    def forward(packed):
        field = unpack(packed, blocks, group).astype(BF16)
        spread = dot(first_wide[...], field).reshape(group, 2, blocks, width)
        re, im = spread[:, 0], spread[:, 1]
        turned = jnp.concatenate([re * mix_re - im * mix_im, re * mix_im + im * mix_re], axis=2)
        return dot(turned.reshape(group * blocks, 2 * width).astype(BF16), lane_ref[...])

    def backward(spectrum):
        spread = dot(spectrum.astype(BF16), lane_back_ref[...]).reshape(group, blocks, 2 * width)
        re, im = spread[:, :, :width], spread[:, :, width:]
        turned = jnp.concatenate([re * mix_re + im * mix_im, im * mix_re - re * mix_im], axis=1)
        return dot(last_wide[...], turned.reshape(2 * group * blocks, width).astype(BF16))

    a2a_wait(out_a, in_a, 0)
    spec_x[...] = forward(in_a[:, : 2 * group])
    spec_f[...] = forward(in_a[:, 2 * group :])
    out_c[...] = pack(backward(product(spec_f[...], spec_x[...], False)), seq, group).astype(BF16)
    a2a_start(out_c, in_c, 2)

    a2a_wait(out_g, in_g, 1)
    spec_g = forward(in_g[...])
    grad_input = pack(backward(product(spec_f[...], spec_g, True)), seq, group)
    grad_taps = pack(backward(product(spec_x[...], spec_g, True)) * scale, seq, group)
    out_d[...] = jnp.concatenate([grad_input, grad_taps], axis=1).astype(BF16)
    a2a_start(out_d, in_d, 3)

    a2a_wait(out_c, in_c, 2)
    conv = unpack(in_c[...], seq, group).T
    grad_query_ref[...] = (grad_query_ref[...].astype(F32) * conv).astype(BF16)
    gated_out = (query_ref[...].astype(F32) * conv).astype(BF16)
    for block in range(mps):
        share = dot(cots_t[block], gated_out).astype(BF16)
        share = share.reshape(per_block, 2, 2, quad_rows, gated_out.shape[1])
        for pair in range(2):
            for core in range(2):
                part[core, pair, pl.ds(block * per_block, per_block)] = share[:, pair, core]

    my_core, my_pair = lax.rem(quad, 2), quad // 2
    to_core = remote(part.at[1 - my_core], core_in, r_send.at[0], r_core, on_seq(core_peer))
    to_core.start()
    to_core.wait_recv()
    pair_out[...] = (
        part[my_core, 1 - my_pair].astype(F32) + core_in[1 - my_pair].astype(F32)
    ).astype(BF16)
    to_pair = remote(pair_out, pair_in, r_send.at[1], r_pair, on_seq(pair_peer))
    to_pair.start()
    both = part[my_core, my_pair].astype(F32) + core_in[my_pair].astype(F32)
    to_pair.wait_recv()
    mine[...] = both + pair_in[...].astype(F32)

    def chain_down(step):
        return remote(down_out.at[step], down_in.at[step], r_send.at[2], r_down.at[step], on_seq(down))

    def chain_up(step):
        return remote(up_out.at[step], up_in.at[step], r_send.at[3], r_up.at[step], on_seq(up))

    for step in range(half):
        held = mine[lax.rem(z + depth - half + step, depth)]
        if step > 0:
            chain_down(step - 1).wait_recv()
            held = held + down_in[step - 1].astype(F32)
        down_out[step] = held.astype(BF16)
        chain_down(step).start()
        if step < half - 1:
            held = mine[lax.rem(z + half - 1 - step, depth)]
            if step > 0:
                chain_up(step - 1).wait_recv()
                held = held + up_in[step - 1].astype(F32)
            up_out[step] = held.astype(BF16)
            chain_up(step).start()
    chain_down(half - 1).wait_recv()
    last_sum = mine[z] + down_in[half - 1].astype(F32)
    if half > 1:
        chain_up(half - 2).wait_recv()
        last_sum = last_sum + up_in[half - 2].astype(F32)
    grad_weight_ref[...] = last_sum * scale

    a2a_wait(out_d, in_d, 3)
    grad_in = unpack(in_d[:, : 2 * group], seq, group).T
    grad_key_ref[...] = (grad_in * value_ref[...].astype(F32)).astype(BF16)
    grad_value_ref[...] = (grad_in * key_ref[...].astype(F32)).astype(BF16)
    grad_filter_ref[...] = unpack(in_d[:, 2 * group :], seq, group).T.astype(BF16)

    for index, source in enumerate((out_a, out_g, out_c, out_d)):
        a2a_sent(source, index)
    whole_wait(weights.at[pl.ds(0, half), quad], w_send.at[0])
    if half > 1:
        whole_wait(weights.at[pl.ds(0, half - 1), quad], w_send.at[1])
    whole_wait(weights.at[:, quad], w_send.at[2])
    core_copy(quad, 0).wait_send()
    core_copy(pair_quad, 1).wait_send()
    for slot in range(2 * columns - 1):
        whole_wait(cots.at[0], cot_send.at[slot])
    to_core.wait_send()
    to_pair.wait_send()
    whole_wait(down_out, r_send.at[2])
    if half > 1:
        whole_wait(up_out, r_send.at[3])


def shards(query_branch, key_branch, value_branch, long_filter, cotangent, out_weight):
    tokens, channels = query_branch.shape
    seq, mps = lax.axis_size("seq"), lax.axis_size("mp")
    depth, half, columns = seq // QUAD, seq // QUAD // 2, mps // 2
    group = channels // seq
    rows, features = out_weight.shape[0], cotangent.shape[1]
    spread = seq * group
    sizes = (seq, mps, seq, tokens, group)
    consts = tables(seq, tokens, group)
    vmem, dma = pltpu.VMEM, pltpu.SemaphoreType.DMA
    wide, single = (seq, 4 * group, tokens // 2), (seq, 2 * group, tokens // 2)
    scratch = [
        vmem(wide, BF16), vmem(wide, BF16), vmem(single, BF16), vmem(single, BF16),
        vmem(single, BF16), vmem(single, BF16), vmem(wide, BF16), vmem(wide, BF16),
        vmem((2 * spread, spread), BF16), vmem((spread, 2 * spread), BF16),
        vmem((spread, 2 * tokens), F32), vmem((spread, 2 * tokens), F32),
        vmem((depth, QUAD, rows, channels), BF16),
        vmem((mps, tokens, features), BF16), vmem((mps, features, tokens), BF16),
        vmem((2, 2, depth, rows, channels), BF16), vmem((2, depth, rows, channels), BF16),
        vmem((depth, rows, channels), BF16), vmem((depth, rows, channels), BF16),
        vmem((depth, rows, channels), F32),
        vmem((half, rows, channels), BF16), vmem((half, rows, channels), BF16),
        vmem((max(half - 1, 1), rows, channels), BF16), vmem((max(half - 1, 1), rows, channels), BF16),
        dma((4, 3)), dma((5,)), dma((half,)), dma((half,)), dma((1,)), dma((2,)),
        dma((2 * columns,)), dma((1,)), dma((columns,)), dma((columns,)),
        dma((4,)), dma(()), dma(()), dma((half,)), dma((half,)),
    ]
    field = jax.ShapeDtypeStruct((tokens, channels), BF16)
    in_vmem = pl.BlockSpec(memory_space=vmem)
    return pl.pallas_call(
        functools.partial(body, sizes),
        out_shape=(field, field, field, field, jax.ShapeDtypeStruct((rows, channels), F32)),
        in_specs=[in_vmem] * 12,
        out_specs=(in_vmem,) * 5,
        scratch_shapes=scratch,
        name="hyena_backward",
        compiler_params=pltpu.CompilerParams(
            collective_id=0, has_side_effects=True, vmem_limit_bytes=56 * 1024 * 1024
        ),
    )(query_branch, key_branch, value_branch, long_filter, cotangent, out_weight, *consts)


def solution(mesh):
    spec = P("seq", "mp")
    return jax.shard_map(
        shards, mesh=mesh, in_specs=(spec,) * 6, out_specs=(spec,) * 5, check_vma=False
    )
```

```python
import functools
import math

import jax
import jax.numpy as jnp
import numpy as np
from jax import lax
from jax.experimental import pallas as pl
from jax.experimental.pallas import tpu as pltpu
from jax.sharding import PartitionSpec as P

MESH = pl.DeviceIdType.MESH
BF16 = jnp.bfloat16
F32 = jnp.float32
QUAD = 4
RING_SHARE = 0.7
FIRST_SHARE = 0.3


def tables(blocks, width, group):
    points = blocks * width
    block = np.arange(blocks)
    lane = np.arange(width)
    turn_block = 2.0 * np.pi * (np.outer(block, 4 * block + 1) % (4 * blocks)) / (4 * blocks)
    turn_mix = 2.0 * np.pi * np.outer(4 * block + 1, lane) / (4 * points)
    turn_lane = 2.0 * np.pi * (np.outer(lane, lane) % width) / width
    cos_l, sin_l = np.cos(turn_lane), np.sin(turn_lane)
    first = np.concatenate([np.cos(turn_block.T), -np.sin(turn_block.T)], axis=0)
    last = np.concatenate([np.cos(turn_block), -np.sin(turn_block)], axis=1) / points
    return (
        jnp.asarray(np.repeat(first, group, axis=1), F32),
        jnp.asarray(np.repeat(last, group, axis=0), F32),
        jnp.asarray(np.cos(turn_mix), F32),
        jnp.asarray(-np.sin(turn_mix), F32),
        jnp.asarray(np.block([[cos_l, -sin_l], [sin_l, cos_l]]), BF16),
        jnp.asarray(np.block([[cos_l, sin_l], [-sin_l, cos_l]]), BF16),
    )


def dot(left, right):
    return jnp.dot(left, right, preferred_element_type=F32)


def pack(field, blocks, group):
    half = field.shape[1] // 2
    shaped = field.reshape(blocks, group, 2 * half)
    return jnp.concatenate([shaped[:, :, :half], shaped[:, :, half:]], axis=1)


def unpack(packed, blocks, group):
    wide = packed.astype(F32)
    joined = jnp.concatenate([wide[:, :group], wide[:, group:]], axis=2)
    return joined.reshape(blocks * group, joined.shape[2])


def product(left, right, conjugate):
    width = left.shape[1] // 2
    left_re, left_im = left[:, :width], left[:, width:]
    right_re, right_im = right[:, :width], right[:, width:]
    if conjugate:
        return jnp.concatenate(
            [left_re * right_re + left_im * right_im, left_re * right_im - left_im * right_re], axis=1
        )
    return jnp.concatenate(
        [left_re * right_re - left_im * right_im, left_re * right_im + left_im * right_re], axis=1
    )


def body(
    sizes,
    query_ref, key_ref, value_ref, filter_ref, cot_ref, weight_ref,
    first_ref, last_ref, mix_re_ref, mix_im_ref, lane_ref, lane_back_ref,
    grad_query_ref, in_d, grad_weight_ref,
    out_a, in_a, out_g, in_g, out_c, in_c, out_d,
    first_wide, last_wide, spec_f, spec_x,
    weights, cots, cots_t, part, core_in, pair_out, pair_in, sums_out, sums_in,
    a2a_sems, w_send, w_ring, w_pair, w_core, cot_send, cot_pair, cot_near, cot_far,
    r_send, r_core, r_pair, r_sums,
):
    seq, mps, blocks, width, group = sizes
    depth = seq // QUAD
    half = depth // 2
    columns = mps // 2
    scale = 1.0 / math.sqrt(blocks * width)
    me, mp = lax.axis_index("seq"), lax.axis_index("mp")
    z, quad = me // QUAD, lax.rem(me, QUAD)
    my_core, my_pair = lax.rem(quad, 2), quad // 2
    core_peer = me + 1 - 2 * my_core
    pair_quad = lax.rem(quad + 2, QUAD)
    pair_peer = z * QUAD + pair_quad
    hops = half // 2

    def on_seq(peer):
        return (peer, mp)

    def on_mp(peer):
        return (me, peer)

    def along_z(offset):
        return lax.rem(z + depth + offset, depth)

    def remote(source, target, send, receive, device):
        return pltpu.make_async_remote_copy(
            src_ref=source, dst_ref=target, send_sem=send, recv_sem=receive,
            device_id=device, device_id_type=MESH,
        )

    def whole_wait(ref, sem):
        pltpu.make_async_copy(ref, ref, sem).wait()

    barrier = pltpu.get_barrier_semaphore()

    @pl.loop(0, seq - 1, unroll=unrolled(seq - 1))
    def _(step):
        pl.semaphore_signal(
            barrier, inc=1, device_id=on_seq(lax.rem(me + step + 1, seq)), device_id_type=MESH
        )

    @pl.loop(0, mps - 1, unroll=mps - 1)
    def _(step):
        pl.semaphore_signal(
            barrier, inc=1, device_id=on_mp(lax.rem(mp + step + 1, mps)), device_id_type=MESH
        )

    def a2a_own(source, target, index):
        return pltpu.make_async_copy(source.at[me], target.at[me], a2a_sems.at[index, 2])

    def a2a_part(source, target, index, begin, end):
        if begin == end:
            return

        @pl.loop(begin, end, unroll=unrolled(end - begin))
        def _(step):
            back = seq - 2 - step
            away = back // 2 + 1
            offset = jnp.where(lax.rem(back, 2) == 0, away, seq - away)
            peer = lax.rem(me + offset, seq)
            remote(
                source.at[peer], target.at[me], a2a_sems.at[index, 0], a2a_sems.at[index, 1], on_seq(peer)
            ).start()

    def a2a_cut(shares):
        work = np.cumsum([1.0 + (seq - 2 - step) // 2 for step in range(seq - 1)])
        ends = np.searchsorted(work / work[-1], np.cumsum(shares) - 1e-6)
        return [0] + [min(int(end) + 1, seq - 1) for end in ends[:-1]] + [seq - 1]

    def a2a_start(source, target, index):
        a2a_own(source, target, index).start()
        a2a_part(source, target, index, 0, seq - 1)

    def a2a_wait(source, target, index):
        a2a_own(source, target, index).wait()
        rest = pl.ds(0, seq - 1)
        pltpu.make_async_copy(target.at[rest], target.at[rest], a2a_sems.at[index, 1]).wait()

    def a2a_sent(source, index):
        rest = pl.ds(0, seq - 1)
        pltpu.make_async_copy(source.at[rest], source.at[rest], a2a_sems.at[index, 0]).wait()

    gated = (key_ref[...].astype(F32) * value_ref[...].astype(F32)).astype(BF16).astype(F32)
    taps = filter_ref[...].astype(F32)
    out_a[...] = jnp.concatenate(
        [pack(gated.T, seq, group), pack(taps.T, seq, group)], axis=1
    ).astype(BF16)
    weights[z, quad] = weight_ref[...]
    cots[mp] = cot_ref[...]

    pl.semaphore_wait(barrier, seq - 1 + mps - 1)

    def at_z(offset):
        return on_seq(along_z(offset) * QUAD + quad)

    def ring(step, sign, reach):
        at = weights.at[along_z(-2 * sign * step), quad]
        way = 0 if sign > 0 else 1
        return remote(at, at, w_send.at[way], w_ring.at[way, step, reach - 1], at_z(sign * reach))

    def ring_reaches(step, sign):
        return (2, 1) if sign > 0 or step + 1 < hops else (1,)

    def pair_copy(origin):
        at = weights.at[origin, quad]
        return remote(at, at, w_send.at[2], w_pair.at[0], on_seq(pair_peer))

    def core_copy(origin):
        at = weights.at[origin, quad]
        return remote(at, at, w_send.at[3], w_core.at[0], on_seq(core_peer))

    def core_rest():
        at = weights.at[:, pair_quad]
        return remote(at, at, w_send.at[4], w_core.at[1], on_seq(core_peer))

    def cot_copy(block, peer, send, receive):
        return remote(cots.at[block], cots.at[block], send, receive, on_mp(peer))

    mp_pair = mp + 1 - 2 * lax.rem(mp, 2)

    def spread_tables():
        rows = 2 * blocks
        lane_group = lax.rem(lax.broadcasted_iota(jnp.int32, (rows, blocks * group), 1), group)
        row_group = lax.rem(lax.broadcasted_iota(jnp.int32, (blocks * group, rows), 0), group)
        for channel in range(group):
            first_wide[pl.ds(channel * rows, rows), :] = jnp.where(
                lane_group == channel, first_ref[...], 0.0
            ).astype(BF16)
            last_wide[:, pl.ds(channel * rows, rows)] = jnp.where(
                row_group == channel, last_ref[...], 0.0
            ).astype(BF16)

    def turn_cots(block):
        per_block = depth // mps
        turned = cots[block].astype(F32).T.astype(BF16)
        cots_t[pl.ds(block * per_block, per_block)] = turned.reshape(
            per_block, turned.shape[0] // per_block, turned.shape[1]
        )

    def ring_start(step):
        for reach in (2, 1):
            for sign in (1, -1):
                if reach in ring_reaches(step, sign):
                    ring(step, sign, reach).start()

    def spread_rows(origin):
        pair_copy(origin).start()
        core_copy(origin).start()

    cut = a2a_cut([RING_SHARE / hops] * hops + [1.0 - RING_SHARE])
    ring_start(0)
    cot_copy(mp, mp_pair, cot_send.at[0], cot_pair.at[0]).start()
    for hop in range(columns - 1):
        peer = lax.rem(mp + 2 * (hop + 1), mps)
        cot_copy(mp, peer, cot_send.at[1 + hop], cot_near.at[hop]).start()
    spread_rows(z)
    a2a_own(out_a, in_a, 0).start()
    for step in range(hops):
        a2a_part(out_a, in_a, 0, cut[step], cut[step + 1])
        if step == 0:
            spread_tables()
        if step == min(1, hops - 1):
            cot_copy(mp, mp_pair, cot_send.at[0], cot_pair.at[0]).wait_recv()
            for hop in range(columns - 1):
                peer = lax.rem(mp + 2 * (hop + 1), mps)
                cot_copy(mp_pair, peer, cot_send.at[columns + hop], cot_far.at[hop]).start()
        if step == hops - 1:
            for hop in range(columns - 1):
                cot_copy(mp, mp, cot_send.at[1 + hop], cot_near.at[hop]).wait_recv()
                cot_copy(mp, mp, cot_send.at[columns + hop], cot_far.at[hop]).wait_recv()
            for block in range(mps):
                turn_cots(block)
        for sign in (1, -1):
            if 2 in ring_reaches(step, sign):
                ring(step, sign, 2).wait_recv()
        if step + 1 < hops:
            ring_start(step + 1)
        for sign in (1, -1):
            ring(step, sign, 1).wait_recv()
            for reach in ring_reaches(step, sign):
                spread_rows(along_z(-sign * (2 * step + reach)))
    a2a_part(out_a, in_a, 0, cut[hops], seq - 1)

    whole_wait(weights.at[:, pair_quad], w_pair.at[0])
    core_rest().start()
    whole_wait(weights.at[:, quad], w_core.at[0])
    core_rest().wait_recv()
    features = cots.shape[2]
    quad_rows = weights.shape[2]
    per_block = features // (QUAD * quad_rows)
    total = jnp.zeros(query_ref.shape, F32)
    for block in range(mps):
        piece = weights[pl.ds(block * per_block, per_block)].reshape(features, query_ref.shape[1])
        total = total + dot(cots[block], piece)
    grad_gated = total.astype(BF16).astype(F32)
    grad_query_ref[...] = grad_gated.astype(BF16)
    query = query_ref[...].astype(F32)
    grad_conv = (grad_gated * query).astype(BF16).astype(F32)
    out_g[...] = pack(grad_conv.T, seq, group).astype(BF16)
    a2a_start(out_g, in_g, 1)

    mix_re, mix_im = mix_re_ref[...], mix_im_ref[...]

    def forward(packed):
        field = unpack(packed, blocks, group).astype(BF16)
        spread = dot(first_wide[...], field).reshape(group, 2, blocks, width)
        re, im = spread[:, 0], spread[:, 1]
        turned = jnp.concatenate([re * mix_re - im * mix_im, re * mix_im + im * mix_re], axis=2)
        return dot(turned.reshape(group * blocks, 2 * width).astype(BF16), lane_ref[...])

    def backward(spectrum):
        spread = dot(spectrum.astype(BF16), lane_back_ref[...]).reshape(group, blocks, 2 * width)
        re, im = spread[:, :, :width], spread[:, :, width:]
        turned = jnp.concatenate([re * mix_re + im * mix_im, im * mix_re - re * mix_im], axis=1)
        return dot(last_wide[...], turned.reshape(2 * group * blocks, width).astype(BF16))

    a2a_wait(out_a, in_a, 0)
    spec_x[...] = forward(in_a[:, : 2 * group])
    spec_f[...] = forward(in_a[:, 2 * group :])
    out_c[...] = pack(backward(product(spec_f[...], spec_x[...], False)), seq, group).astype(BF16)
    a2a_start(out_c, in_c, 2)

    a2a_wait(out_g, in_g, 1)
    spec_g = forward(in_g[...])
    grad_input = pack(backward(product(spec_f[...], spec_g, True)), seq, group)
    grad_taps = pack(backward(product(spec_x[...], spec_g, True)) * scale, seq, group)
    out_d[...] = jnp.concatenate([grad_input, grad_taps], axis=1).astype(BF16)
    cut = a2a_cut([FIRST_SHARE] + [(1.0 - FIRST_SHARE) / (half - 1)] * (half - 1))
    a2a_own(out_d, in_d, 3).start()
    a2a_part(out_d, in_d, 3, 0, cut[1])

    a2a_wait(out_c, in_c, 2)
    conv = unpack(in_c[...], seq, group).T
    grad_query_ref[...] = (grad_query_ref[...].astype(F32) * conv).astype(BF16)
    gated_out = (query_ref[...].astype(F32) * conv).astype(BF16)

    offsets = [half] + [sign * away for away in range(half - 1, 0, -1) for sign in (-1, 1)] + [0]
    order = [along_z(offset) for offset in offsets]

    def to_core(slot):
        block = order[slot]
        return remote(
            part.at[1 - my_core, :, block], core_in.at[:, block],
            r_send.at[0], r_core.at[slot], on_seq(core_peer),
        )

    def to_pair(slot):
        block = order[slot]
        return remote(
            pair_out.at[block], pair_in.at[block], r_send.at[1], r_pair.at[slot], on_seq(pair_peer)
        )

    for slot in range(depth):
        share = dot(cots_t[order[slot]], gated_out).astype(BF16)
        share = share.reshape(2, 2, quad_rows, gated_out.shape[1])
        for pair in range(2):
            for core in range(2):
                part[core, pair, order[slot]] = share[pair, core]
        to_core(slot).start()
    for slot in range(depth):
        to_core(slot).wait_recv()
        pair_out[order[slot]] = (
            part[my_core, 1 - my_pair, order[slot]].astype(F32)
            + core_in[1 - my_pair, order[slot]].astype(F32)
        ).astype(BF16)
        to_pair(slot).start()

    def of_chip_pair(slot):
        to_pair(slot).wait_recv()
        block = order[slot]
        return (
            part[my_core, my_pair, block].astype(F32)
            + core_in[my_pair, block].astype(F32)
            + pair_in[block].astype(F32)
        )

    def chain(away, sign, reach):
        way = 0 if sign < 0 else 1
        return remote(
            sums_out.at[way, away - 1], sums_in.at[way, reach - 1, away // 2],
            r_send.at[2 + way], r_sums.at[way, reach - 1, away // 2], at_z(sign * reach),
        )

    def arrived(away, sign):
        behind = 0.0
        farthest = half if sign < 0 else half - 1
        for reach in (1, 2):
            if away + reach <= farthest:
                chain(away + reach, sign, reach).wait_recv()
                way = 0 if sign < 0 else 1
                behind = behind + sums_in[way, reach - 1, (away + reach) // 2].astype(F32)
        return behind

    def chain_send(slot, away, sign):
        held = of_chip_pair(slot)
        if away % 2 == 0:
            held = held + arrived(away, sign)
        way = 0 if sign < 0 else 1
        sums_out[way, away - 1] = held.astype(BF16)
        chain(away, sign, 2 - away % 2).start()

    chain_send(0, half, -1)
    for away in range(half - 1, 0, -1):
        for side, sign in enumerate((-1, 1)):
            chain_send(1 + 2 * (half - 1 - away) + side, away, sign)
        step = half - 1 - away
        a2a_part(out_d, in_d, 3, cut[step + 1], cut[step + 2])
    last_sum = of_chip_pair(depth - 1) + arrived(0, -1) + arrived(0, 1)
    grad_weight_ref[...] = last_sum * scale
    a2a_wait(out_d, in_d, 3)

    for index, source in enumerate((out_a, out_g, out_c, out_d)):
        a2a_sent(source, index)
    whole_wait(weights.at[pl.ds(0, half), quad], w_send.at[0])
    whole_wait(weights.at[pl.ds(0, half - 1), quad], w_send.at[1])
    whole_wait(weights.at[:, quad], w_send.at[2])
    whole_wait(weights.at[:, quad], w_send.at[3])
    core_rest().wait_send()
    for slot in range(2 * columns - 1):
        whole_wait(cots.at[0], cot_send.at[slot])
    whole_wait(core_in, r_send.at[0])
    whole_wait(pair_out, r_send.at[1])
    whole_wait(sums_out.at[0], r_send.at[2])
    whole_wait(sums_out.at[1, pl.ds(0, half - 1)], r_send.at[3])


def finish(sizes, packed_ref, key_ref, value_ref, query_in, weight_in, key_out, value_out, filter_out, query_out, weight_out):
    group = sizes[-1]
    peers = packed_ref.shape[0]
    grad_in = unpack(packed_ref[:, : 2 * group], peers, group).T
    key_out[...] = (grad_in * value_ref[...].astype(F32)).astype(BF16)
    value_out[...] = (grad_in * key_ref[...].astype(F32)).astype(BF16)
    filter_out[...] = unpack(packed_ref[:, 2 * group :], peers, group).T.astype(BF16)
    query_out[...] = query_in[...]
    weight_out[...] = weight_in[...]


def unrolled(count):
    return max(part for part in range(1, 10) if count % part == 0)


def shards(query_branch, key_branch, value_branch, long_filter, cotangent, out_weight):
    tokens, channels = query_branch.shape
    seq, mps = lax.axis_size("seq"), lax.axis_size("mp")
    depth, half, columns = seq // QUAD, seq // QUAD // 2, mps // 2
    group = channels // seq
    rows, features = out_weight.shape[0], cotangent.shape[1]
    spread = seq * group
    sizes = (seq, mps, seq, tokens, group)
    consts = tables(seq, tokens, group)
    vmem, dma = pltpu.VMEM, pltpu.SemaphoreType.DMA
    wide, single = (seq, 4 * group, tokens // 2), (seq, 2 * group, tokens // 2)
    scratch = [
        vmem(wide, BF16), vmem(wide, BF16), vmem(single, BF16), vmem(single, BF16),
        vmem(single, BF16), vmem(single, BF16), vmem(wide, BF16),
        vmem((2 * spread, spread), BF16), vmem((spread, 2 * spread), BF16),
        vmem((spread, 2 * tokens), F32), vmem((spread, 2 * tokens), F32),
        vmem((depth, QUAD, rows, channels), BF16),
        vmem((mps, tokens, features), BF16), vmem((depth, QUAD * rows, tokens), BF16),
        vmem((2, 2, depth, rows, channels), BF16), vmem((2, depth, rows, channels), BF16),
        vmem((depth, rows, channels), BF16), vmem((depth, rows, channels), BF16),
        vmem((2, half, rows, channels), BF16), vmem((2, 2, half // 2 + 1, rows, channels), BF16),
        dma((4, 3)), dma((5,)), dma((2, half // 2, 2)), dma((1,)), dma((2,)),
        dma((2 * columns,)), dma((1,)), dma((columns,)), dma((columns,)),
        dma((4,)), dma((depth,)), dma((depth,)), dma((2, 2, half // 2 + 1)),
    ]
    field = jax.ShapeDtypeStruct((tokens, channels), BF16)
    weight = jax.ShapeDtypeStruct((rows, channels), F32)
    in_vmem = pl.BlockSpec(memory_space=vmem)
    grad_query, packed, grad_weight = pl.pallas_call(
        functools.partial(body, sizes),
        out_shape=(field, jax.ShapeDtypeStruct(wide, BF16), weight),
        in_specs=[in_vmem] * 12,
        out_specs=(in_vmem,) * 3,
        scratch_shapes=scratch,
        name="hyena_backward",
        compiler_params=pltpu.CompilerParams(
            collective_id=0, has_side_effects=True, vmem_limit_bytes=56 * 1024 * 1024
        ),
    )(query_branch, key_branch, value_branch, long_filter, cotangent, out_weight, *consts)
    pieces = 2
    column = pl.BlockSpec((tokens, channels // pieces), lambda piece: (0, piece))
    thin = pl.BlockSpec((rows, channels // pieces), lambda piece: (0, piece))
    peers = pl.BlockSpec((seq // pieces,) + wide[1:], lambda piece: (piece, 0, 0))
    grad_key, grad_value, grad_filter, grad_query, grad_weight = pl.pallas_call(
        functools.partial(finish, sizes),
        grid=(pieces,),
        out_shape=(field, field, field, field, weight),
        in_specs=[peers, column, column, column, thin],
        out_specs=(column, column, column, column, thin),
        name="gate_gradients",
    )(packed, key_branch, value_branch, grad_query, grad_weight)
    return grad_query, grad_key, grad_value, grad_filter, grad_weight


def solution(mesh):
    spec = P("seq", "mp")
    return jax.shard_map(
        shards, mesh=mesh, in_specs=(spec,) * 6, out_specs=(spec,) * 5, check_vma=False
    )
```

```python
import functools
import math

import jax
import jax.numpy as jnp
import numpy as np
from jax import lax
from jax.experimental import pallas as pl
from jax.experimental.pallas import tpu as pltpu
from jax.sharding import PartitionSpec as P

MESH = pl.DeviceIdType.MESH
BF16 = jnp.bfloat16
F32 = jnp.float32
QUAD = 4
RING_SHARE = 0.7
FIRST_SHARE = 0.9
STEP_SHARE = 0.03


def tables(blocks, width, group):
    points = blocks * width
    block = np.arange(blocks)
    lane = np.arange(width)
    turn_block = 2.0 * np.pi * (np.outer(block, 4 * block + 1) % (4 * blocks)) / (4 * blocks)
    turn_mix = 2.0 * np.pi * np.outer(4 * block + 1, lane) / (4 * points)
    turn_lane = 2.0 * np.pi * (np.outer(lane, lane) % width) / width
    cos_l, sin_l = np.cos(turn_lane), np.sin(turn_lane)
    first = np.concatenate([np.cos(turn_block.T), -np.sin(turn_block.T)], axis=0)
    last = np.concatenate([np.cos(turn_block), -np.sin(turn_block)], axis=1) / points
    return (
        jnp.asarray(np.repeat(first, group, axis=1), F32),
        jnp.asarray(np.repeat(last, group, axis=0), F32),
        jnp.asarray(np.cos(turn_mix), F32),
        jnp.asarray(-np.sin(turn_mix), F32),
        jnp.asarray(np.block([[cos_l, -sin_l], [sin_l, cos_l]]), BF16),
        jnp.asarray(np.block([[cos_l, sin_l], [-sin_l, cos_l]]), BF16),
    )


def dot(left, right):
    return jnp.dot(left, right, preferred_element_type=F32)


def pack(field, blocks, group):
    half = field.shape[1] // 2
    shaped = field.reshape(blocks, group, 2 * half)
    return jnp.concatenate([shaped[:, :, :half], shaped[:, :, half:]], axis=1)


def unpack(packed, blocks, group):
    wide = packed.astype(F32)
    joined = jnp.concatenate([wide[:, :group], wide[:, group:]], axis=2)
    return joined.reshape(blocks * group, joined.shape[2])


def product(left, right, conjugate):
    width = left.shape[1] // 2
    left_re, left_im = left[:, :width], left[:, width:]
    right_re, right_im = right[:, :width], right[:, width:]
    if conjugate:
        return jnp.concatenate(
            [left_re * right_re + left_im * right_im, left_re * right_im - left_im * right_re], axis=1
        )
    return jnp.concatenate(
        [left_re * right_re - left_im * right_im, left_re * right_im + left_im * right_re], axis=1
    )


def body(
    sizes,
    query_ref, key_ref, value_ref, filter_ref, cot_ref, weight_ref,
    first_ref, last_ref, mix_re_ref, mix_im_ref, lane_ref, lane_back_ref,
    grad_query_ref, in_d, grad_weight_ref,
    out_a, in_a, out_g, in_g, out_c, in_c, out_d,
    first_wide, last_wide, spec_f, spec_x,
    weights, cots, cots_t, part, core_in, pair_out, pair_in, sums_out, sums_in,
    a2a_sems, w_send, w_ring, w_pair, w_core, cot_send, cot_pair, cot_near, cot_far,
    r_send, r_core, r_pair, r_sums,
):
    seq, mps, blocks, width, group = sizes
    depth = seq // QUAD
    half = depth // 2
    columns = mps // 2
    scale = 1.0 / math.sqrt(blocks * width)
    me, mp = lax.axis_index("seq"), lax.axis_index("mp")
    z, quad = me // QUAD, lax.rem(me, QUAD)
    my_core, my_pair = lax.rem(quad, 2), quad // 2
    core_peer = me + 1 - 2 * my_core
    pair_quad = lax.rem(quad + 2, QUAD)
    pair_peer = z * QUAD + pair_quad
    hops = half // 2

    def on_seq(peer):
        return (peer, mp)

    def on_mp(peer):
        return (me, peer)

    def along_z(offset):
        return lax.rem(z + depth + offset, depth)

    def remote(source, target, send, receive, device):
        return pltpu.make_async_remote_copy(
            src_ref=source, dst_ref=target, send_sem=send, recv_sem=receive,
            device_id=device, device_id_type=MESH,
        )

    def whole_wait(ref, sem):
        pltpu.make_async_copy(ref, ref, sem).wait()

    barrier = pltpu.get_barrier_semaphore()

    @pl.loop(0, seq - 1, unroll=unrolled(seq - 1))
    def _(step):
        pl.semaphore_signal(
            barrier, inc=1, device_id=on_seq(lax.rem(me + step + 1, seq)), device_id_type=MESH
        )

    @pl.loop(0, mps - 1, unroll=mps - 1)
    def _(step):
        pl.semaphore_signal(
            barrier, inc=1, device_id=on_mp(lax.rem(mp + step + 1, mps)), device_id_type=MESH
        )

    def a2a_own(source, target, index):
        return pltpu.make_async_copy(source.at[me], target.at[me], a2a_sems.at[index, 2])

    def a2a_part(source, target, index, begin, end):
        if begin == end:
            return

        @pl.loop(begin, end, unroll=unrolled(end - begin))
        def _(step):
            back = seq - 2 - step
            away = back // 2 + 1
            offset = jnp.where(lax.rem(back, 2) == 0, away, seq - away)
            peer = lax.rem(me + offset, seq)
            remote(
                source.at[peer], target.at[me], a2a_sems.at[index, 0], a2a_sems.at[index, 1], on_seq(peer)
            ).start()

    def a2a_cut(shares):
        work = np.cumsum([1.0 + (seq - 2 - step) // 2 for step in range(seq - 1)])
        ends = np.searchsorted(work / work[-1], np.cumsum(shares) - 1e-6)
        return [0] + [min(int(end) + 1, seq - 1) for end in ends[:-1]] + [seq - 1]

    def a2a_start(source, target, index):
        a2a_own(source, target, index).start()
        a2a_part(source, target, index, 0, seq - 1)

    def a2a_wait(source, target, index):
        a2a_own(source, target, index).wait()
        rest = pl.ds(0, seq - 1)
        pltpu.make_async_copy(target.at[rest], target.at[rest], a2a_sems.at[index, 1]).wait()

    def a2a_sent(source, index):
        rest = pl.ds(0, seq - 1)
        pltpu.make_async_copy(source.at[rest], source.at[rest], a2a_sems.at[index, 0]).wait()

    gated = (key_ref[...].astype(F32) * value_ref[...].astype(F32)).astype(BF16).astype(F32)
    taps = filter_ref[...].astype(F32)
    out_a[...] = jnp.concatenate(
        [pack(gated.T, seq, group), pack(taps.T, seq, group)], axis=1
    ).astype(BF16)
    weights[z, quad] = weight_ref[...]
    cots[mp] = cot_ref[...]

    pl.semaphore_wait(barrier, seq - 1 + mps - 1)

    def at_z(offset):
        return on_seq(along_z(offset) * QUAD + quad)

    def ring(step, sign, reach):
        at = weights.at[along_z(-2 * sign * step), quad]
        way = 0 if sign > 0 else 1
        return remote(at, at, w_send.at[way], w_ring.at[way, step, reach - 1], at_z(sign * reach))

    def ring_reaches(step, sign):
        return (2, 1) if sign > 0 or step + 1 < hops else (1,)

    def pair_copy(origin):
        at = weights.at[origin, quad]
        return remote(at, at, w_send.at[2], w_pair.at[0], on_seq(pair_peer))

    def core_copy(origin):
        at = weights.at[origin, quad]
        return remote(at, at, w_send.at[3], w_core.at[0], on_seq(core_peer))

    def core_rest():
        at = weights.at[:, pair_quad]
        return remote(at, at, w_send.at[4], w_core.at[1], on_seq(core_peer))

    def cot_copy(block, peer, send, receive):
        return remote(cots.at[block], cots.at[block], send, receive, on_mp(peer))

    mp_pair = mp + 1 - 2 * lax.rem(mp, 2)

    def spread_tables():
        rows = 2 * blocks
        lane_group = lax.rem(lax.broadcasted_iota(jnp.int32, (rows, blocks * group), 1), group)
        row_group = lax.rem(lax.broadcasted_iota(jnp.int32, (blocks * group, rows), 0), group)
        for channel in range(group):
            first_wide[pl.ds(channel * rows, rows), :] = jnp.where(
                lane_group == channel, first_ref[...], 0.0
            ).astype(BF16)
            last_wide[:, pl.ds(channel * rows, rows)] = jnp.where(
                row_group == channel, last_ref[...], 0.0
            ).astype(BF16)

    def turn_cots(block):
        per_block = depth // mps
        turned = cots[block].astype(F32).T.astype(BF16)
        cots_t[pl.ds(block * per_block, per_block)] = turned.reshape(
            per_block, turned.shape[0] // per_block, turned.shape[1]
        )

    def ring_start(step):
        for reach in (2, 1):
            for sign in (1, -1):
                if reach in ring_reaches(step, sign):
                    ring(step, sign, reach).start()

    def spread_rows(origin):
        pair_copy(origin).start()
        core_copy(origin).start()

    cut = a2a_cut([RING_SHARE / hops] * hops + [1.0 - RING_SHARE])
    ring_start(0)
    cot_copy(mp, mp_pair, cot_send.at[0], cot_pair.at[0]).start()
    for hop in range(columns - 1):
        peer = lax.rem(mp + 2 * (hop + 1), mps)
        cot_copy(mp, peer, cot_send.at[1 + hop], cot_near.at[hop]).start()
    spread_rows(z)
    a2a_own(out_a, in_a, 0).start()
    for step in range(hops):
        a2a_part(out_a, in_a, 0, cut[step], cut[step + 1])
        if step == 0:
            spread_tables()
        if step == min(1, hops - 1):
            cot_copy(mp, mp_pair, cot_send.at[0], cot_pair.at[0]).wait_recv()
            for hop in range(columns - 1):
                peer = lax.rem(mp + 2 * (hop + 1), mps)
                cot_copy(mp_pair, peer, cot_send.at[columns + hop], cot_far.at[hop]).start()
        if step == hops - 1:
            for hop in range(columns - 1):
                cot_copy(mp, mp, cot_send.at[1 + hop], cot_near.at[hop]).wait_recv()
                cot_copy(mp, mp, cot_send.at[columns + hop], cot_far.at[hop]).wait_recv()
            for block in range(mps):
                turn_cots(block)
        for sign in (1, -1):
            if 2 in ring_reaches(step, sign):
                ring(step, sign, 2).wait_recv()
        if step + 1 < hops:
            ring_start(step + 1)
        for sign in (1, -1):
            ring(step, sign, 1).wait_recv()
            for reach in ring_reaches(step, sign):
                spread_rows(along_z(-sign * (2 * step + reach)))
    a2a_part(out_a, in_a, 0, cut[hops], seq - 1)

    whole_wait(weights.at[:, pair_quad], w_pair.at[0])
    core_rest().start()
    whole_wait(weights.at[:, quad], w_core.at[0])
    core_rest().wait_recv()
    features = cots.shape[2]
    quad_rows = weights.shape[2]
    per_block = features // (QUAD * quad_rows)
    total = jnp.zeros(query_ref.shape, F32)
    for block in range(mps):
        piece = weights[pl.ds(block * per_block, per_block)].reshape(features, query_ref.shape[1])
        total = total + dot(cots[block], piece)
    grad_gated = total.astype(BF16).astype(F32)
    grad_query_ref[...] = grad_gated.astype(BF16)
    query = query_ref[...].astype(F32)
    grad_conv = (grad_gated * query).astype(BF16).astype(F32)
    out_g[...] = pack(grad_conv.T, seq, group).astype(BF16)
    a2a_start(out_g, in_g, 1)

    mix_re, mix_im = mix_re_ref[...], mix_im_ref[...]

    def forward(packed):
        field = unpack(packed, blocks, group).astype(BF16)
        spread = dot(first_wide[...], field).reshape(group, 2, blocks, width)
        re, im = spread[:, 0], spread[:, 1]
        turned = jnp.concatenate([re * mix_re - im * mix_im, re * mix_im + im * mix_re], axis=2)
        return dot(turned.reshape(group * blocks, 2 * width).astype(BF16), lane_ref[...])

    def backward(spectrum):
        spread = dot(spectrum.astype(BF16), lane_back_ref[...]).reshape(group, blocks, 2 * width)
        re, im = spread[:, :, :width], spread[:, :, width:]
        turned = jnp.concatenate([re * mix_re + im * mix_im, im * mix_re - re * mix_im], axis=1)
        return dot(last_wide[...], turned.reshape(2 * group * blocks, width).astype(BF16))

    a2a_wait(out_a, in_a, 0)
    spec_x[...] = forward(in_a[:, : 2 * group])
    spec_f[...] = forward(in_a[:, 2 * group :])
    out_c[...] = pack(backward(product(spec_f[...], spec_x[...], False)), seq, group).astype(BF16)
    a2a_start(out_c, in_c, 2)

    a2a_wait(out_g, in_g, 1)
    spec_g = forward(in_g[...])
    grad_input = pack(backward(product(spec_f[...], spec_g, True)), seq, group)
    grad_taps = pack(backward(product(spec_x[...], spec_g, True)) * scale, seq, group)
    out_d[...] = jnp.concatenate([grad_input, grad_taps], axis=1).astype(BF16)
    cut = a2a_cut([FIRST_SHARE] + [STEP_SHARE] * (hops - 1) + [1.0 - FIRST_SHARE - STEP_SHARE * (hops - 1)])
    a2a_own(out_d, in_d, 3).start()
    a2a_part(out_d, in_d, 3, 0, cut[1])

    a2a_wait(out_c, in_c, 2)
    conv = unpack(in_c[...], seq, group).T
    grad_query_ref[...] = (grad_query_ref[...].astype(F32) * conv).astype(BF16)
    gated_out = (query_ref[...].astype(F32) * conv).astype(BF16)

    aways = [half, half - 1]
    for away in range(half - 2, 0, -2):
        aways += [away - 1, away]
    offsets = [sign * away for away in aways for sign in ((-1,) if away == half else (-1, 1))] + [0]
    order = [along_z(offset) for offset in offsets]

    def to_core(slot):
        block = order[slot]
        return remote(
            part.at[1 - my_core, :, block], core_in.at[:, block],
            r_send.at[0], r_core.at[slot], on_seq(core_peer),
        )

    def to_pair(slot):
        block = order[slot]
        return remote(
            pair_out.at[block], pair_in.at[block], r_send.at[1], r_pair.at[slot], on_seq(pair_peer)
        )

    for slot in range(depth):
        share = dot(cots_t[order[slot]], gated_out).astype(BF16)
        share = share.reshape(2, 2, quad_rows, gated_out.shape[1])
        for pair in range(2):
            for core in range(2):
                part[core, pair, order[slot]] = share[pair, core]
        to_core(slot).start()
    for slot in range(depth):
        to_core(slot).wait_recv()
        pair_out[order[slot]] = (
            part[my_core, 1 - my_pair, order[slot]].astype(F32)
            + core_in[1 - my_pair, order[slot]].astype(F32)
        ).astype(BF16)
        to_pair(slot).start()

    def of_chip_pair(slot):
        to_pair(slot).wait_recv()
        block = order[slot]
        return (
            part[my_core, my_pair, block].astype(F32)
            + core_in[my_pair, block].astype(F32)
            + pair_in[block].astype(F32)
        )

    def chain(away, sign, reach):
        way = 0 if sign < 0 else 1
        return remote(
            sums_out.at[way, away - 1], sums_in.at[way, reach - 1, away // 2],
            r_send.at[2 + way], r_sums.at[way, reach - 1, away // 2], at_z(sign * reach),
        )

    def arrived(away, sign):
        behind = 0.0
        farthest = half if sign < 0 else half - 1
        for reach in (1, 2):
            if away + reach <= farthest:
                chain(away + reach, sign, reach).wait_recv()
                way = 0 if sign < 0 else 1
                behind = behind + sums_in[way, reach - 1, (away + reach) // 2].astype(F32)
        return behind

    def chain_send(slot, away, sign):
        held = of_chip_pair(slot)
        if away % 2 == 0:
            held = held + arrived(away, sign)
        way = 0 if sign < 0 else 1
        sums_out[way, away - 1] = held.astype(BF16)
        chain(away, sign, 2 - away % 2).start()

    step = 0
    for away in aways:
        for sign in (-1, 1):
            if away < half or sign < 0:
                chain_send(offsets.index(sign * away), away, sign)
        if away == half - 1 or (away % 2 == 0 and away < half):
            a2a_part(out_d, in_d, 3, cut[step + 1], cut[step + 2])
            step += 1
    last_sum = of_chip_pair(depth - 1) + arrived(0, -1) + arrived(0, 1)
    grad_weight_ref[...] = last_sum * scale
    a2a_wait(out_d, in_d, 3)

    for index, source in enumerate((out_a, out_g, out_c, out_d)):
        a2a_sent(source, index)
    whole_wait(weights.at[pl.ds(0, half), quad], w_send.at[0])
    whole_wait(weights.at[pl.ds(0, half - 1), quad], w_send.at[1])
    whole_wait(weights.at[:, quad], w_send.at[2])
    whole_wait(weights.at[:, quad], w_send.at[3])
    core_rest().wait_send()
    for slot in range(2 * columns - 1):
        whole_wait(cots.at[0], cot_send.at[slot])
    whole_wait(core_in, r_send.at[0])
    whole_wait(pair_out, r_send.at[1])
    whole_wait(sums_out.at[0], r_send.at[2])
    whole_wait(sums_out.at[1, pl.ds(0, half - 1)], r_send.at[3])


def finish(sizes, packed_ref, key_ref, value_ref, query_in, weight_in, key_out, value_out, filter_out, query_out, weight_out):
    group = sizes[-1]
    peers = packed_ref.shape[0]
    grad_in = unpack(packed_ref[:, : 2 * group], peers, group).T
    key_out[...] = (grad_in * value_ref[...].astype(F32)).astype(BF16)
    value_out[...] = (grad_in * key_ref[...].astype(F32)).astype(BF16)
    filter_out[...] = unpack(packed_ref[:, 2 * group :], peers, group).T.astype(BF16)
    query_out[...] = query_in[...]
    weight_out[...] = weight_in[...]


def unrolled(count):
    return max(part for part in range(1, 10) if count % part == 0)


def shards(query_branch, key_branch, value_branch, long_filter, cotangent, out_weight):
    tokens, channels = query_branch.shape
    seq, mps = lax.axis_size("seq"), lax.axis_size("mp")
    depth, half, columns = seq // QUAD, seq // QUAD // 2, mps // 2
    group = channels // seq
    rows, features = out_weight.shape[0], cotangent.shape[1]
    spread = seq * group
    sizes = (seq, mps, seq, tokens, group)
    consts = tables(seq, tokens, group)
    vmem, dma = pltpu.VMEM, pltpu.SemaphoreType.DMA
    wide, single = (seq, 4 * group, tokens // 2), (seq, 2 * group, tokens // 2)
    scratch = [
        vmem(wide, BF16), vmem(wide, BF16), vmem(single, BF16), vmem(single, BF16),
        vmem(single, BF16), vmem(single, BF16), vmem(wide, BF16),
        vmem((2 * spread, spread), BF16), vmem((spread, 2 * spread), BF16),
        vmem((spread, 2 * tokens), F32), vmem((spread, 2 * tokens), F32),
        vmem((depth, QUAD, rows, channels), BF16),
        vmem((mps, tokens, features), BF16), vmem((depth, QUAD * rows, tokens), BF16),
        vmem((2, 2, depth, rows, channels), BF16), vmem((2, depth, rows, channels), BF16),
        vmem((depth, rows, channels), BF16), vmem((depth, rows, channels), BF16),
        vmem((2, half, rows, channels), BF16), vmem((2, 2, half // 2 + 1, rows, channels), BF16),
        dma((4, 3)), dma((5,)), dma((2, half // 2, 2)), dma((1,)), dma((2,)),
        dma((2 * columns,)), dma((1,)), dma((columns,)), dma((columns,)),
        dma((4,)), dma((depth,)), dma((depth,)), dma((2, 2, half // 2 + 1)),
    ]
    field = jax.ShapeDtypeStruct((tokens, channels), BF16)
    weight = jax.ShapeDtypeStruct((rows, channels), F32)
    in_vmem = pl.BlockSpec(memory_space=vmem)
    grad_query, packed, grad_weight = pl.pallas_call(
        functools.partial(body, sizes),
        out_shape=(field, jax.ShapeDtypeStruct(wide, BF16), weight),
        in_specs=[in_vmem] * 12,
        out_specs=(in_vmem,) * 3,
        scratch_shapes=scratch,
        name="hyena_backward",
        compiler_params=pltpu.CompilerParams(
            collective_id=0, has_side_effects=True, vmem_limit_bytes=56 * 1024 * 1024
        ),
    )(query_branch, key_branch, value_branch, long_filter, cotangent, out_weight, *consts)
    pieces = 2
    column = pl.BlockSpec((tokens, channels // pieces), lambda piece: (0, piece))
    thin = pl.BlockSpec((rows, channels // pieces), lambda piece: (0, piece))
    peers = pl.BlockSpec((seq // pieces,) + wide[1:], lambda piece: (piece, 0, 0))
    grad_key, grad_value, grad_filter, grad_query, grad_weight = pl.pallas_call(
        functools.partial(finish, sizes),
        grid=(pieces,),
        out_shape=(field, field, field, field, weight),
        in_specs=[peers, column, column, column, thin],
        out_specs=(column, column, column, column, thin),
        name="gate_gradients",
    )(packed, key_branch, value_branch, grad_query, grad_weight)
    return grad_query, grad_key, grad_value, grad_filter, grad_weight


def solution(mesh):
    spec = P("seq", "mp")
    return jax.shard_map(
        shards, mesh=mesh, in_specs=(spec,) * 6, out_specs=(spec,) * 5, check_vma=False
    )
```

```python
import functools
import math

import jax
import jax.numpy as jnp
import numpy as np
from jax import lax
from jax.experimental import pallas as pl
from jax.experimental.pallas import tpu as pltpu
from jax.sharding import PartitionSpec as P

MESH = pl.DeviceIdType.MESH
BF16 = jnp.bfloat16
F32 = jnp.float32
QUAD = 4
RING_SHARE = 0.7
FIRST_SHARE = 0.7


def tables(blocks, width, group):
    points = blocks * width
    block = np.arange(blocks)
    lane = np.arange(width)
    turn_block = 2.0 * np.pi * (np.outer(block, 4 * block + 1) % (4 * blocks)) / (4 * blocks)
    turn_mix = 2.0 * np.pi * np.outer(4 * block + 1, lane) / (4 * points)
    turn_lane = 2.0 * np.pi * (np.outer(lane, lane) % width) / width
    cos_l, sin_l = np.cos(turn_lane), np.sin(turn_lane)
    first = np.concatenate([np.cos(turn_block.T), -np.sin(turn_block.T)], axis=0)
    last = np.concatenate([np.cos(turn_block), -np.sin(turn_block)], axis=1) / points
    return (
        jnp.asarray(np.repeat(first, group, axis=1), F32),
        jnp.asarray(np.repeat(last, group, axis=0), F32),
        jnp.asarray(np.cos(turn_mix), F32),
        jnp.asarray(-np.sin(turn_mix), F32),
        jnp.asarray(np.block([[cos_l, -sin_l], [sin_l, cos_l]]), BF16),
        jnp.asarray(np.block([[cos_l, sin_l], [-sin_l, cos_l]]), BF16),
    )


def dot(left, right):
    return jnp.dot(left, right, preferred_element_type=F32)


def pack(field, blocks, group):
    half = field.shape[1] // 2
    shaped = field.reshape(blocks, group, 2 * half)
    return jnp.concatenate([shaped[:, :, :half], shaped[:, :, half:]], axis=1)


def unpack(packed, blocks, group):
    wide = packed.astype(F32)
    joined = jnp.concatenate([wide[:, :group], wide[:, group:]], axis=2)
    return joined.reshape(blocks * group, joined.shape[2])


def product(left, right, conjugate):
    width = left.shape[1] // 2
    left_re, left_im = left[:, :width], left[:, width:]
    right_re, right_im = right[:, :width], right[:, width:]
    if conjugate:
        return jnp.concatenate(
            [left_re * right_re + left_im * right_im, left_re * right_im - left_im * right_re], axis=1
        )
    return jnp.concatenate(
        [left_re * right_re - left_im * right_im, left_re * right_im + left_im * right_re], axis=1
    )


def body(
    sizes,
    query_ref, key_ref, value_ref, filter_ref, cot_ref, weight_ref,
    first_ref, last_ref, mix_re_ref, mix_im_ref, lane_ref, lane_back_ref,
    grad_query_ref, in_d, grad_weight_ref,
    out_a, in_a, out_g, in_g, out_c, in_c, out_d,
    first_wide, last_wide, spec_f, spec_x,
    weights, cots, cots_t, part, core_in, pair_out, pair_in, sums_out, sums_in,
    a2a_sems, w_send, w_ring, w_pair, w_core, cot_send, cot_pair, cot_near, cot_far,
    r_send, r_core, r_pair, r_sums,
):
    seq, mps, blocks, width, group = sizes
    depth = seq // QUAD
    half = depth // 2
    columns = mps // 2
    scale = 1.0 / math.sqrt(blocks * width)
    me, mp = lax.axis_index("seq"), lax.axis_index("mp")
    z, quad = me // QUAD, lax.rem(me, QUAD)
    my_core, my_pair = lax.rem(quad, 2), quad // 2
    core_peer = me + 1 - 2 * my_core
    pair_quad = lax.rem(quad + 2, QUAD)
    pair_peer = z * QUAD + pair_quad
    hops = half // 2

    def on_seq(peer):
        return (peer, mp)

    def on_mp(peer):
        return (me, peer)

    def along_z(offset):
        return lax.rem(z + depth + offset, depth)

    def remote(source, target, send, receive, device):
        return pltpu.make_async_remote_copy(
            src_ref=source, dst_ref=target, send_sem=send, recv_sem=receive,
            device_id=device, device_id_type=MESH,
        )

    def whole_wait(ref, sem):
        pltpu.make_async_copy(ref, ref, sem).wait()

    barrier = pltpu.get_barrier_semaphore()

    @pl.loop(0, seq - 1, unroll=unrolled(seq - 1))
    def _(step):
        pl.semaphore_signal(
            barrier, inc=1, device_id=on_seq(lax.rem(me + step + 1, seq)), device_id_type=MESH
        )

    @pl.loop(0, mps - 1, unroll=mps - 1)
    def _(step):
        pl.semaphore_signal(
            barrier, inc=1, device_id=on_mp(lax.rem(mp + step + 1, mps)), device_id_type=MESH
        )

    def a2a_own(source, target, index):
        return pltpu.make_async_copy(source.at[me], target.at[me], a2a_sems.at[index, 2])

    def a2a_part(source, target, index, begin, end):
        if begin == end:
            return

        @pl.loop(begin, end, unroll=unrolled(end - begin))
        def _(step):
            back = seq - 2 - step
            away = back // 2 + 1
            offset = jnp.where(lax.rem(back, 2) == 0, away, seq - away)
            peer = lax.rem(me + offset, seq)
            remote(
                source.at[peer], target.at[me], a2a_sems.at[index, 0], a2a_sems.at[index, 1], on_seq(peer)
            ).start()

    def a2a_cut(shares):
        work = np.cumsum([1.0 + (seq - 2 - step) // 2 for step in range(seq - 1)])
        ends = np.searchsorted(work / work[-1], np.cumsum(shares) - 1e-6)
        return [0] + [min(int(end) + 1, seq - 1) for end in ends[:-1]] + [seq - 1]

    def a2a_start(source, target, index):
        a2a_own(source, target, index).start()
        a2a_part(source, target, index, 0, seq - 1)

    def a2a_wait(source, target, index):
        a2a_own(source, target, index).wait()
        rest = pl.ds(0, seq - 1)
        pltpu.make_async_copy(target.at[rest], target.at[rest], a2a_sems.at[index, 1]).wait()

    def a2a_sent(source, index):
        rest = pl.ds(0, seq - 1)
        pltpu.make_async_copy(source.at[rest], source.at[rest], a2a_sems.at[index, 0]).wait()

    gated = (key_ref[...].astype(F32) * value_ref[...].astype(F32)).astype(BF16).astype(F32)
    taps = filter_ref[...].astype(F32)
    out_a[...] = jnp.concatenate(
        [pack(gated.T, seq, group), pack(taps.T, seq, group)], axis=1
    ).astype(BF16)
    weights[z, quad] = weight_ref[...]
    cots[mp] = cot_ref[...]

    pl.semaphore_wait(barrier, seq - 1 + mps - 1)

    def at_z(offset):
        return on_seq(along_z(offset) * QUAD + quad)

    def ring(step, sign, reach):
        at = weights.at[along_z(-2 * sign * step), quad]
        way = 0 if sign > 0 else 1
        return remote(at, at, w_send.at[way], w_ring.at[way, step, reach - 1], at_z(sign * reach))

    def ring_reaches(step, sign):
        return (2, 1) if sign > 0 or step + 1 < hops else (1,)

    def pair_copy(origin):
        at = weights.at[origin, quad]
        return remote(at, at, w_send.at[2], w_pair.at[0], on_seq(pair_peer))

    def core_copy(origin):
        at = weights.at[origin, quad]
        return remote(at, at, w_send.at[3], w_core.at[0], on_seq(core_peer))

    def core_rest():
        at = weights.at[:, pair_quad]
        return remote(at, at, w_send.at[4], w_core.at[1], on_seq(core_peer))

    def cot_copy(block, peer, send, receive):
        return remote(cots.at[block], cots.at[block], send, receive, on_mp(peer))

    mp_pair = mp + 1 - 2 * lax.rem(mp, 2)

    def spread_tables():
        rows = 2 * blocks
        lane_group = lax.rem(lax.broadcasted_iota(jnp.int32, (rows, blocks * group), 1), group)
        row_group = lax.rem(lax.broadcasted_iota(jnp.int32, (blocks * group, rows), 0), group)
        for channel in range(group):
            first_wide[pl.ds(channel * rows, rows), :] = jnp.where(
                lane_group == channel, first_ref[...], 0.0
            ).astype(BF16)
            last_wide[:, pl.ds(channel * rows, rows)] = jnp.where(
                row_group == channel, last_ref[...], 0.0
            ).astype(BF16)

    def turn_cots(block):
        per_block = depth // mps
        turned = cots[block].astype(F32).T.astype(BF16)
        cots_t[pl.ds(block * per_block, per_block)] = turned.reshape(
            per_block, turned.shape[0] // per_block, turned.shape[1]
        )

    def ring_start(step):
        for reach in (2, 1):
            for sign in (1, -1):
                if reach in ring_reaches(step, sign):
                    ring(step, sign, reach).start()

    def spread_rows(origin):
        pair_copy(origin).start()
        core_copy(origin).start()

    grow = [RING_SHARE * (step + 1.5) / (hops * (hops + 2) / 2) for step in range(hops)]
    cut = a2a_cut(grow + [1.0 - RING_SHARE])
    ring_start(0)
    cot_copy(mp, mp_pair, cot_send.at[0], cot_pair.at[0]).start()
    for hop in range(columns - 1):
        peer = lax.rem(mp + 2 * (hop + 1), mps)
        cot_copy(mp, peer, cot_send.at[1 + hop], cot_near.at[hop]).start()
    spread_rows(z)
    a2a_own(out_a, in_a, 0).start()
    for step in range(hops):
        a2a_part(out_a, in_a, 0, cut[step], cut[step + 1])
        if step == 0:
            spread_tables()
        if step == min(1, hops - 1):
            cot_copy(mp, mp_pair, cot_send.at[0], cot_pair.at[0]).wait_recv()
            for hop in range(columns - 1):
                peer = lax.rem(mp + 2 * (hop + 1), mps)
                cot_copy(mp_pair, peer, cot_send.at[columns + hop], cot_far.at[hop]).start()
        if step == hops - 1:
            for hop in range(columns - 1):
                cot_copy(mp, mp, cot_send.at[1 + hop], cot_near.at[hop]).wait_recv()
                cot_copy(mp, mp, cot_send.at[columns + hop], cot_far.at[hop]).wait_recv()
            for block in range(mps):
                turn_cots(block)
        for sign in (1, -1):
            if 2 in ring_reaches(step, sign):
                ring(step, sign, 2).wait_recv()
        if step + 1 < hops:
            ring_start(step + 1)
        for sign in (1, -1):
            ring(step, sign, 1).wait_recv()
            for reach in ring_reaches(step, sign):
                spread_rows(along_z(-sign * (2 * step + reach)))
    a2a_part(out_a, in_a, 0, cut[hops], seq - 1)

    whole_wait(weights.at[:, pair_quad], w_pair.at[0])
    core_rest().start()
    whole_wait(weights.at[:, quad], w_core.at[0])
    core_rest().wait_recv()
    features = cots.shape[2]
    quad_rows = weights.shape[2]
    per_block = features // (QUAD * quad_rows)
    total = jnp.zeros(query_ref.shape, F32)
    for block in range(mps):
        piece = weights[pl.ds(block * per_block, per_block)].reshape(features, query_ref.shape[1])
        total = total + dot(cots[block], piece)
    grad_gated = total.astype(BF16).astype(F32)
    grad_query_ref[...] = grad_gated.astype(BF16)
    query = query_ref[...].astype(F32)
    grad_conv = (grad_gated * query).astype(BF16).astype(F32)
    out_g[...] = pack(grad_conv.T, seq, group).astype(BF16)
    a2a_start(out_g, in_g, 1)

    mix_re, mix_im = mix_re_ref[...], mix_im_ref[...]

    def forward(packed):
        field = unpack(packed, blocks, group).astype(BF16)
        spread = dot(first_wide[...], field).reshape(group, 2, blocks, width)
        re, im = spread[:, 0], spread[:, 1]
        turned = jnp.concatenate([re * mix_re - im * mix_im, re * mix_im + im * mix_re], axis=2)
        return dot(turned.reshape(group * blocks, 2 * width).astype(BF16), lane_ref[...])

    def backward(spectrum):
        spread = dot(spectrum.astype(BF16), lane_back_ref[...]).reshape(group, blocks, 2 * width)
        re, im = spread[:, :, :width], spread[:, :, width:]
        turned = jnp.concatenate([re * mix_re + im * mix_im, im * mix_re - re * mix_im], axis=1)
        return dot(last_wide[...], turned.reshape(2 * group * blocks, width).astype(BF16))

    a2a_wait(out_a, in_a, 0)
    spec_x[...] = forward(in_a[:, : 2 * group])
    spec_f[...] = forward(in_a[:, 2 * group :])
    out_c[...] = pack(backward(product(spec_f[...], spec_x[...], False)), seq, group).astype(BF16)
    a2a_start(out_c, in_c, 2)

    a2a_wait(out_g, in_g, 1)
    spec_g = forward(in_g[...])
    grad_input = pack(backward(product(spec_f[...], spec_g, True)), seq, group)
    grad_taps = pack(backward(product(spec_x[...], spec_g, True)) * scale, seq, group)
    out_d[...] = jnp.concatenate([grad_input, grad_taps], axis=1).astype(BF16)
    cut = a2a_cut([FIRST_SHARE, 1.0 - FIRST_SHARE])
    a2a_own(out_d, in_d, 3).start()
    a2a_part(out_d, in_d, 3, 0, cut[1])

    a2a_wait(out_c, in_c, 2)
    conv = unpack(in_c[...], seq, group).T
    grad_query_ref[...] = (grad_query_ref[...].astype(F32) * conv).astype(BF16)
    gated_out = (query_ref[...].astype(F32) * conv).astype(BF16)

    aways = [half, half - 1]
    for away in range(half - 2, 0, -2):
        aways += [away - 1, away]
    offsets = [sign * away for away in aways for sign in ((-1,) if away == half else (-1, 1))] + [0]
    order = [along_z(offset) for offset in offsets]

    def to_core(slot):
        block = order[slot]
        return remote(
            part.at[1 - my_core, :, block], core_in.at[:, block],
            r_send.at[0], r_core.at[slot], on_seq(core_peer),
        )

    def to_pair(slot):
        block = order[slot]
        return remote(
            pair_out.at[block], pair_in.at[block], r_send.at[1], r_pair.at[slot], on_seq(pair_peer)
        )

    for slot in range(depth):
        share = dot(cots_t[order[slot]], gated_out).astype(BF16)
        share = share.reshape(2, 2, quad_rows, gated_out.shape[1])
        for pair in range(2):
            for core in range(2):
                part[core, pair, order[slot]] = share[pair, core]
        to_core(slot).start()
    for slot in range(depth):
        to_core(slot).wait_recv()
        pair_out[order[slot]] = (
            part[my_core, 1 - my_pair, order[slot]].astype(F32)
            + core_in[1 - my_pair, order[slot]].astype(F32)
        ).astype(BF16)
        to_pair(slot).start()

    def of_chip_pair(slot):
        to_pair(slot).wait_recv()
        block = order[slot]
        return (
            part[my_core, my_pair, block].astype(F32)
            + core_in[my_pair, block].astype(F32)
            + pair_in[block].astype(F32)
        )

    def chain(away, sign, reach):
        way = 0 if sign < 0 else 1
        return remote(
            sums_out.at[way, away - 1], sums_in.at[way, reach - 1, away // 2],
            r_send.at[2 + way], r_sums.at[way, reach - 1, away // 2], at_z(sign * reach),
        )

    def arrived(away, sign):
        behind = 0.0
        farthest = half if sign < 0 else half - 1
        for reach in (1, 2):
            if away + reach <= farthest:
                chain(away + reach, sign, reach).wait_recv()
                way = 0 if sign < 0 else 1
                behind = behind + sums_in[way, reach - 1, (away + reach) // 2].astype(F32)
        return behind

    def chain_send(slot, away, sign):
        held = of_chip_pair(slot)
        if away % 2 == 0:
            held = held + arrived(away, sign)
        way = 0 if sign < 0 else 1
        sums_out[way, away - 1] = held.astype(BF16)
        chain(away, sign, 2 - away % 2).start()

    for away in aways:
        for sign in (-1, 1):
            if away < half or sign < 0:
                chain_send(offsets.index(sign * away), away, sign)
        if away == half - 1:
            a2a_part(out_d, in_d, 3, cut[1], seq - 1)
    last_sum = of_chip_pair(depth - 1) + arrived(0, -1) + arrived(0, 1)
    grad_weight_ref[...] = last_sum * scale
    a2a_wait(out_d, in_d, 3)

    for index, source in enumerate((out_a, out_g, out_c, out_d)):
        a2a_sent(source, index)
    whole_wait(weights.at[pl.ds(0, half), quad], w_send.at[0])
    whole_wait(weights.at[pl.ds(0, half - 1), quad], w_send.at[1])
    whole_wait(weights.at[:, quad], w_send.at[2])
    whole_wait(weights.at[:, quad], w_send.at[3])
    core_rest().wait_send()
    for slot in range(2 * columns - 1):
        whole_wait(cots.at[0], cot_send.at[slot])
    whole_wait(core_in, r_send.at[0])
    whole_wait(pair_out, r_send.at[1])
    whole_wait(sums_out.at[0], r_send.at[2])
    whole_wait(sums_out.at[1, pl.ds(0, half - 1)], r_send.at[3])


def finish(sizes, packed_ref, key_ref, value_ref, query_in, weight_in, key_out, value_out, filter_out, query_out, weight_out):
    group = sizes[-1]
    peers = packed_ref.shape[0]
    grad_in = unpack(packed_ref[:, : 2 * group], peers, group).T
    key_out[...] = (grad_in * value_ref[...].astype(F32)).astype(BF16)
    value_out[...] = (grad_in * key_ref[...].astype(F32)).astype(BF16)
    filter_out[...] = unpack(packed_ref[:, 2 * group :], peers, group).T.astype(BF16)
    query_out[...] = query_in[...]
    weight_out[...] = weight_in[...]


def unrolled(count):
    return max(part for part in range(1, 10) if count % part == 0)


def shards(query_branch, key_branch, value_branch, long_filter, cotangent, out_weight):
    tokens, channels = query_branch.shape
    seq, mps = lax.axis_size("seq"), lax.axis_size("mp")
    depth, half, columns = seq // QUAD, seq // QUAD // 2, mps // 2
    group = channels // seq
    rows, features = out_weight.shape[0], cotangent.shape[1]
    spread = seq * group
    sizes = (seq, mps, seq, tokens, group)
    consts = tables(seq, tokens, group)
    vmem, dma = pltpu.VMEM, pltpu.SemaphoreType.DMA
    wide, single = (seq, 4 * group, tokens // 2), (seq, 2 * group, tokens // 2)
    scratch = [
        vmem(wide, BF16), vmem(wide, BF16), vmem(single, BF16), vmem(single, BF16),
        vmem(single, BF16), vmem(single, BF16), vmem(wide, BF16),
        vmem((2 * spread, spread), BF16), vmem((spread, 2 * spread), BF16),
        vmem((spread, 2 * tokens), F32), vmem((spread, 2 * tokens), F32),
        vmem((depth, QUAD, rows, channels), BF16),
        vmem((mps, tokens, features), BF16), vmem((depth, QUAD * rows, tokens), BF16),
        vmem((2, 2, depth, rows, channels), BF16), vmem((2, depth, rows, channels), BF16),
        vmem((depth, rows, channels), BF16), vmem((depth, rows, channels), BF16),
        vmem((2, half, rows, channels), BF16), vmem((2, 2, half // 2 + 1, rows, channels), BF16),
        dma((4, 3)), dma((5,)), dma((2, half // 2, 2)), dma((1,)), dma((2,)),
        dma((2 * columns,)), dma((1,)), dma((columns,)), dma((columns,)),
        dma((4,)), dma((depth,)), dma((depth,)), dma((2, 2, half // 2 + 1)),
    ]
    field = jax.ShapeDtypeStruct((tokens, channels), BF16)
    weight = jax.ShapeDtypeStruct((rows, channels), F32)
    in_vmem = pl.BlockSpec(memory_space=vmem)
    grad_query, packed, grad_weight = pl.pallas_call(
        functools.partial(body, sizes),
        out_shape=(field, jax.ShapeDtypeStruct(wide, BF16), weight),
        in_specs=[in_vmem] * 12,
        out_specs=(in_vmem,) * 3,
        scratch_shapes=scratch,
        name="hyena_backward",
        compiler_params=pltpu.CompilerParams(
            collective_id=0, has_side_effects=True, vmem_limit_bytes=56 * 1024 * 1024
        ),
    )(query_branch, key_branch, value_branch, long_filter, cotangent, out_weight, *consts)
    pieces = 2
    column = pl.BlockSpec((tokens, channels // pieces), lambda piece: (0, piece))
    thin = pl.BlockSpec((rows, channels // pieces), lambda piece: (0, piece))
    peers = pl.BlockSpec((seq // pieces,) + wide[1:], lambda piece: (piece, 0, 0))
    grad_key, grad_value, grad_filter, grad_query, grad_weight = pl.pallas_call(
        functools.partial(finish, sizes),
        grid=(pieces,),
        out_shape=(field, field, field, field, weight),
        in_specs=[peers, column, column, column, thin],
        out_specs=(column, column, column, column, thin),
        name="gate_gradients",
    )(packed, key_branch, value_branch, grad_query, grad_weight)
    return grad_query, grad_key, grad_value, grad_filter, grad_weight


def solution(mesh):
    spec = P("seq", "mp")
    return jax.shard_map(
        shards, mesh=mesh, in_specs=(spec,) * 6, out_specs=(spec,) * 5, check_vma=False
    )
```
